32 devices in a mesh: lev: 2 (over x), gx: 8 (over z, y), gy: 2 (over core).
Axes of the slice: x: 2, y: 2, z: 4, core: 2. Of those that a mesh axis runs over, the one named last changes fastest.
Arguments:
- increments: float32 [1, 2, 80, 128, 256], P(None, None, 'lev', 'gx', 'gy'), may hold values from -6 to 6
- vert_corr: float32 [2, 80, 80], replicated, may hold values from -0.025 to 1, as said below
- kappa: float32 [2, 128, 256], P(None, 'gx', 'gy'), may hold values from 0.03 to 0.24
- sea_mask: int32 [80, 128, 256], P('lev', 'gx', 'gy'), may hold values 0 or 1
- level_count: int32 [128, 256], P('gx', 'gy'), may hold values from 10 to 75
Outputs:
- covaried: float32 [1, 2, 80, 128, 256], P(None, None, 'lev', 'gx', 'gy')
The draws below stay inside these ranges and needn't reach their ends.
Inputs may be any that keep to these rules, and one draw needn't show every extreme that they name: vert_corr has ones on the diagonal, and each row's other entries together have magnitude below one.
All inputs are finite; a program needn't handle non-finite values. No bound on the sum of `sea_mask` on one device may be relied on, other than what follows from the above.
Results may differ from the reference program's by a relative error of at most 0.00021.
Values sent between devices are 32-bit elements; how exact they have to be, the bound alone decides.
A program may use at most 64 MiB of HBM per device.

```python
import math
import jax
import jax.numpy as jnp
from jax import lax

LEV = 80
TRACERS = 2
PASSES = 10
DIRS = 1
NX = 128
NY = 256


def draw_vert_corr(key, part):
    key_one = jax.random.fold_in(jax.random.fold_in(key, 17), 0)
    noise = jax.random.uniform(key_one, (TRACERS, LEV, LEV), jnp.float32, -1.0, 1.0)
    offdiag = noise * (1.2 / LEV)
    index = jnp.arange(LEV)
    diagonal = (index[:, None] == index[None, :])[None]
    return jnp.where(diagonal, 1.0, offdiag).astype(jnp.float32)


def plant(drawn, key, least, top_value):
    spot = [jax.random.randint(jax.random.fold_in(key, axis), (), 0, length) for axis, length in enumerate(drawn.shape)]
    widest = drawn.shape.index(max(drawn.shape))
    next_to = spot[:widest] + [(spot[widest] + 1) % drawn.shape[widest]] + spot[widest + 1:]
    return drawn.at[tuple(spot)].set(least).at[tuple(next_to)].set(top_value)


def shard_levels(stream_key, dims, shards, least, high):
    factor_of = 1.0
    for position, shards_of in shards:
        heights = jax.random.uniform(jax.random.fold_in(jax.random.fold_in(stream_key, 6), position), (shards_of,), jnp.float32, least / len(shards), high / len(shards))
        factor_of = factor_of * jnp.repeat(jnp.exp(heights), dims[position] // shards_of).reshape((-1,) + (1,) * (len(dims) - 1 - position))
    return factor_of


def normal_values(stream_key, dims, deviation, reach, cuts=(), held_as=jnp.bfloat16):
    loudness = shard_levels(stream_key, dims, cuts, -0.22, 0.18) if cuts else 1.0
    entries = jax.random.normal(stream_key, dims, jnp.float32) * deviation * loudness
    return jnp.minimum(jnp.maximum(entries, -reach), reach).astype(held_as)


def setup_inputs(seed: int = 0) -> dict:
    key_of = jax.random.split(jax.random.key(seed), 6)
    return {
        "increments": normal_values(key_of[0], (DIRS, TRACERS, LEV, NX, NY), 1.0, 6.0, ((2, 2), (3, 8), (4, 2)), jnp.float32),
        "vert_corr": draw_vert_corr(jax.random.fold_in(key_of[5], 71), 0),
        "kappa": jnp.clip(jnp.exp(math.log(0.24) - 2.0794415 * jax.random.uniform(key_of[2], (2, NX, NY), jnp.float32) ** shard_levels(key_of[2], (2, NX, NY), ((1, 8), (2, 2)), -0.2, 0.2)), 0.03, 0.24),
        "sea_mask": plant((jax.random.randint(key_of[3], (LEV, NX, NY), 0, 10) < 9).astype(jnp.int32), jax.random.fold_in(key_of[3], 1), 0, 1),
        "level_count": plant(jax.random.randint(key_of[4], (NX, NY), LEV // 8, LEV - LEV // 16 + 1), jax.random.fold_in(key_of[4], 1), LEV // 8, (LEV - LEV // 16 + 1) - 1).astype(jnp.int32),
    }


def reference(increments, vert_corr, kappa, sea_mask, level_count):
    levels = jnp.arange(LEV, dtype=jnp.int32)
    wet = (sea_mask * (levels[:, None, None] < level_count[None]).astype(jnp.int32)).astype(jnp.float32)
    east = kappa[0]
    north = kappa[1] * (jnp.arange(NY, dtype=jnp.int32) != NY - 1).astype(jnp.float32)[None, :]
    east_back = jnp.roll(east, 1, 0)
    north_back = jnp.roll(north, 1, 1)
    fields = increments.reshape(DIRS * TRACERS, LEV, NX, NY)
    tracer_ids = jnp.tile(jnp.arange(TRACERS, dtype=jnp.int32), DIRS)

    def apply_one(item):
        field, tracer = item
        matrix = vert_corr[tracer]
        masked = field * wet
        result = jnp.einsum("oh,hxy->oxy", matrix, masked, precision=lax.Precision.HIGHEST) * wet
        for step in range(PASSES):
            flux = east * (jnp.roll(result, -1, 1) - result) + east_back * (jnp.roll(result, 1, 1) - result)
            flux = flux + north * (jnp.roll(result, -1, 2) - result) + north_back * (jnp.roll(result, 1, 2) - result)
            result = wet * (result + flux)
        return result

    output = lax.map(apply_one, (fields, tracer_ids))
    return output.reshape(increments.shape)
```

```python
import jax
import jax.numpy as jnp
from jax import lax
from jax.experimental import pallas as pl
from jax.experimental.pallas import tpu as pltpu
from jax.sharding import PartitionSpec as P

PASSES = 10


def from_behind(block, axis, distance):
    devices = range(lax.axis_size(axis))
    route = [((i - distance) % len(devices), i) for i in devices]
    return lax.ppermute(block, axis, route)


def shifted(block, axis, distance):
    devices = range(lax.axis_size(axis))
    route = [(i - distance, i) for i in devices if i - distance in devices]
    return lax.ppermute(block, axis, route)


def padded(cells, sides, width):
    for axis, dim in sides:
        count = lax.axis_size(axis)
        head = lax.slice_in_dim(cells, 0, width, axis=dim)
        tail = lax.slice_in_dim(cells, cells.shape[dim] - width, cells.shape[dim], axis=dim)
        cells = jnp.concatenate(
            [
                lax.ppermute(tail, axis, [(i, (i + 1) % count) for i in range(count)]),
                cells,
                lax.ppermute(head, axis, [((i + 1) % count, i) for i in range(count)]),
            ],
            axis=dim,
        )
    return cells


def relax(extended, east_ext, north_ext, wet_center):
    center = extended[..., 1:-1, 1:-1]
    flux = east_ext[1:-1, 1:-1] * (extended[..., 2:, 1:-1] - center)
    flux = flux + east_ext[:-2, 1:-1] * (extended[..., :-2, 1:-1] - center)
    flux = flux + north_ext[1:-1, 1:-1] * (extended[..., 1:-1, 2:] - center)
    flux = flux + north_ext[1:-1, :-2] * (extended[..., 1:-1, :-2] - center)
    return wet_center * (center + flux)


def per_device(increments, vert_corr, kappa, sea_mask, level_count):
    lev_dev = sea_mask.shape[0]
    cells_x = sea_mask.shape[1]
    cells_y = sea_mask.shape[2]
    lev_first = lax.axis_index("lev") * lev_dev
    levels = lev_first + jnp.arange(lev_dev, dtype=jnp.int32)
    wet = sea_mask * (levels[:, None, None] < level_count[None]).astype(jnp.int32)
    wet_float = wet.astype(jnp.float32)
    masked = increments * wet_float
    own_rows = lax.dynamic_slice_in_dim(vert_corr, lev_first, lev_dev, 1)
    correlated = jnp.einsum(
        "toh,dthxy->dtoxy",
        own_rows,
        lax.all_gather(masked, "lev", axis=2, tiled=True),
        precision=lax.Precision.HIGHEST,
    )
    field = correlated * wet_float
    total_y = cells_y * lax.axis_size("gy")
    local_rows = lax.axis_index("gy") * cells_y + jnp.arange(cells_y, dtype=jnp.int32)
    open_local = (local_rows != total_y - 1).astype(jnp.float32)
    east_local = kappa[0]
    north_local = kappa[1] * open_local[None, :]
    east_low = from_behind(east_local[-1:, :], "gx", 1)
    north_low = shifted(north_local[:, -1:], "gy", 1)
    zero_row = jnp.zeros((1, cells_y), jnp.float32)
    zero_col = jnp.zeros((cells_x, 1), jnp.float32)
    east_ext = jnp.pad(jnp.concatenate([east_low, east_local, zero_row], axis=0), ((0, 0), (1, 1)))
    north_ext = jnp.pad(
        jnp.concatenate([north_low, north_local, zero_col], axis=1), ((1, 1), (0, 0))
    )

    def one_pass(step, current):
        extended = padded(current, (("gx", 3), ("gy", 4)), 1)
        return relax(extended, east_ext, north_ext, wet_float)

    field = lax.fori_loop(0, PASSES, one_pass, field)
    return field


TILE = 8
LANES = 128
WIDTH = 5
MESH = pl.DeviceIdType.MESH


def remote(src, dst, send_sem, recv_sem, device):
    return pltpu.make_async_remote_copy(
        src_ref=src,
        dst_ref=dst,
        send_sem=send_sem,
        recv_sem=recv_sem,
        device_id=device,
        device_id_type=MESH,
    )


def kernel(
    masked_ref, wet_ref, corr_ref, kappa_ref, out_ref,
    geo, own, other, field, halo, east, north, south,
    own_sems, same_sems, cross_sems, geo_sems, halo_sems, out_sems,
):
    lev, gx, gy = lax.axis_index("lev"), lax.axis_index("gx"), lax.axis_index("gy")
    count = lax.axis_size("gx")
    cells = masked_ref.shape[1]
    levels = masked_ref.shape[2]
    lanes = masked_ref.shape[3]
    tiles = levels // TILE
    width = WIDTH
    rows = cells + 2 * width
    rounds = PASSES // width
    east_dev = {"gx": lax.rem(gx + 1, count)}
    west_dev = {"gx": lax.rem(gx + count - 1, count)}
    mate = {"gy": 1 - gy}
    pair = {"lev": 1 - lev}
    cross = {"lev": 1 - lev, "gy": 1 - gy}

    barrier = pltpu.get_barrier_semaphore()
    everyone = (east_dev, west_dev, mate, pair, cross)
    for device in everyone:
        pl.semaphore_signal(barrier, inc=1, device_id=device, device_id_type=MESH)
    columns = gy * lanes + lax.broadcasted_iota(jnp.int32, (1, lanes), 1)
    is_open = (columns != lanes * lax.axis_size("gy") - 1).astype(jnp.float32)
    geo[gy, width:width + cells, 0:levels] = wet_ref[...]
    for x in range(cells):
        geo[gy, width + x, levels:levels + 1] = kappa_ref[0, x:x + 1]
        geo[gy, width + x, levels + 1:levels + 2] = kappa_ref[1, x:x + 1] * is_open
        geo[gy, width + x, levels + 2:] = jnp.zeros((TILE - 2, lanes), jnp.float32)
    pl.semaphore_wait(barrier, len(everyone))

    starts = ((0, width), (cells - width, width), (width, cells - 2 * width))
    own_copies, same_copies, cross_copies = [], [], []
    for q, (start, size) in enumerate(starts):
        span = pl.ds(start, size)
        own_copies.append(remote(
            masked_ref.at[1 - gy, span], own.at[span], own_sems.at[0, q], own_sems.at[1, q], mate))
        same_copies.append(remote(
            masked_ref.at[gy, span], other.at[gy, span],
            same_sems.at[0, q], same_sems.at[1, q], pair))
        cross_copies.append(remote(
            masked_ref.at[1 - gy, span], other.at[gy, span],
            cross_sems.at[0, q], cross_sems.at[1, q], cross))
    geo_copies = [
        remote(geo.at[gy, pl.ds(width, cells)], geo.at[gy, pl.ds(width, cells)], geo_sems.at[0, 0], geo_sems.at[1, 0], mate),
        remote(geo.at[gy, pl.ds(cells, width)],
               geo.at[gy, pl.ds(0, width)],
               geo_sems.at[0, 1], geo_sems.at[1, 1], east_dev),
        remote(geo.at[gy, pl.ds(width, width)],
               geo.at[gy, pl.ds(width + cells, width)],
               geo_sems.at[0, 2], geo_sems.at[1, 2], west_dev),
    ]
    for q in range(len(starts)):
        same_copies[q].start()
        cross_copies[q].start()
        if q == 0:
            for copy in geo_copies[1:]:
                copy.start()
            geo_copies[0].start()
        own_copies[q].start()

    mine = corr_ref[gy, pl.ds(pl.multiple_of(lev * levels, TILE), levels), :]
    swapped = jnp.concatenate([mine[:, levels:], mine[:, :levels]], axis=1)
    corr = jnp.where(lev == 0, mine, swapped)
    high = corr.astype(jnp.bfloat16)
    low = (corr - high.astype(jnp.float32)).astype(jnp.bfloat16)
    weights = jnp.concatenate([high, high, low], axis=1)

    def halo_copies(r, k):
        return (
            remote(field.at[k, pl.ds(width, width)], halo.at[r, 1, k],
                   halo_sems.at[0, r, 0, k], halo_sems.at[1, r, 0, k], west_dev),
            remote(field.at[k, pl.ds(cells, width)], halo.at[r, 0, k],
                   halo_sems.at[0, r, 1, k], halo_sems.at[1, r, 1, k], east_dev),
        )

    def vertical(x):
        mine = masked_ref[gy, x]
        theirs = own[x]
        first = jnp.where(gy == 0, mine, theirs)
        second = jnp.where(gy == 0, theirs, mine)
        near = jnp.concatenate([first, second], axis=1)
        far = jnp.concatenate([other[0, x], other[1, x]], axis=1)
        both = jnp.concatenate([near, far], axis=0)
        top = both.astype(jnp.bfloat16)
        rest = (both - top.astype(jnp.float32)).astype(jnp.bfloat16)
        stack = jnp.concatenate([top, rest, top], axis=0)
        result = jnp.dot(weights, stack, preferred_element_type=jnp.float32)
        for half in range(2):
            for k in range(tiles):
                value = result[k * TILE:(k + 1) * TILE, half * LANES:(half + 1) * LANES]
                wet = geo[half, width + x, k * TILE:(k + 1) * TILE]
                field[k, width + x, half] = value * wet

    pending = [halo_copies(0, k) for k in range(tiles)]
    forward = []
    geo_copies[0].wait()
    for q, (start, size) in enumerate(starts):
        own_copies[q].wait()
        same_copies[q].wait()
        cross_copies[q].wait()
        for x in range(start, start + size):
            vertical(x)
        if q < 2:
            for k in range(tiles):
                pending[k][q].start()
        if q == 1:
            for side, place in ((1, 0), (2, width + cells)):
                geo_copies[side].wait()
                edge = geo.at[gy, pl.ds(place, width)]
                forward.append(remote(
                    edge, edge, geo_sems.at[0, 2 + side], geo_sems.at[1, 2 + side], mate))
                forward[-1].start()
    for copy in forward:
        copy.wait()
    for half in range(2):
        for row in range(rows):
            east[row, half] = jnp.broadcast_to(geo[half, row, levels:levels + 1], (TILE, LANES))
            north[row, half] = jnp.broadcast_to(geo[half, row, levels + 1:levels + 2], (TILE, LANES))

    lane = lax.broadcasted_iota(jnp.int32, (TILE, LANES), 1)
    at_end = lane == LANES - 1
    at_start = lane == 0
    for row in range(rows):
        moved = [pltpu.roll(north[row, h], 1, 1) for h in range(2)]
        south[row, 0] = jnp.where(at_start, moved[1], moved[0])
        south[row, 1] = jnp.where(at_start, moved[0], moved[1])

    def relax_tile(r, k):
        for step in range(width):
            def row_of(row):
                if step == 0 and row < width:
                    return halo[r, 0, k, row, 0], halo[r, 0, k, row, 1]
                if step == 0 and row >= width + cells:
                    at = row - width - cells
                    return halo[r, 1, k, at, 0], halo[r, 1, k, at, 1]
                return field[k, row, 0], field[k, row, 1]

            first, last = step + 1, rows - 2 - step
            before, here = row_of(first - 1), row_of(first)
            flux = [east[first - 1, h] * (here[h] - before[h]) for h in range(2)]
            for row in range(first, last + 1):
                after = row_of(row + 1)
                turned = [pltpu.roll(here[h], LANES - 1, 1) for h in range(2)]
                up = [jnp.where(at_end, turned[1], turned[0]), turned[1]]
                back = [pltpu.roll(here[h], 1, 1) for h in range(2)]
                below = [back[0], jnp.where(at_start, back[0], back[1])]
                rise = [north[row, h] * (up[h] - here[h]) for h in range(2)]
                down = [south[row, h] * (here[h] - below[h]) for h in range(2)]
                ahead = [east[row, h] * (after[h] - here[h]) for h in range(2)]
                for h in range(2):
                    wet = geo[h, row, k * TILE:(k + 1) * TILE]
                    total = here[h] + ((ahead[h] - flux[h]) + (rise[h] - down[h]))
                    field[k, row, h] = wet * total
                here, flux = after, ahead

    out_copies = []
    for r in range(rounds):
        later = []
        for k in range(tiles):
            for copy in pending[k]:
                copy.wait()
            relax_tile(r, k)
            if r < rounds - 1:
                later.append(halo_copies(r + 1, k))
                for copy in later[-1]:
                    copy.start()
            else:
                out_copies.append(remote(
                    field.at[k, pl.ds(width, cells), 1 - gy], out_ref.at[gy, k],
                    out_sems.at[0, k], out_sems.at[1, k], mate))
                out_copies[-1].start()
                out_ref[gy, k] = field[k, width:width + cells, gy]
        pending = later
    for copy in out_copies:
        copy.wait()


def fused(increments, vert_corr, kappa, sea_mask, level_count):
    levels, cells, lanes = sea_mask.shape
    tiles = levels // TILE
    width = WIDTH
    rows = cells + 2 * width
    rounds = PASSES // width
    lev = lax.axis_index("lev")
    numbers = lev * levels + jnp.arange(levels, dtype=jnp.int32)
    turned = jnp.swapaxes(sea_mask, 0, 1)
    wet = (turned * (numbers[None, :, None] < level_count[:, None, :]).astype(jnp.int32)).astype(jnp.float32)
    masked = jnp.swapaxes(increments[0], 1, 2) * wet[None]
    vmem = pl.BlockSpec(memory_space=pltpu.VMEM)
    f32 = jnp.float32
    dma = pltpu.SemaphoreType.DMA
    result = pl.pallas_call(
        kernel,
        out_shape=jax.ShapeDtypeStruct((2, tiles, cells, TILE, lanes), f32),
        in_specs=[vmem] * 4,
        out_specs=vmem,
        scratch_shapes=[
            pltpu.VMEM((2, rows, levels + TILE, lanes), f32),
            pltpu.VMEM((cells, levels, lanes), f32),
            pltpu.VMEM((2, cells, levels, lanes), f32),
            pltpu.VMEM((tiles, rows, 2, TILE, lanes), f32),
            pltpu.VMEM((rounds, 2, tiles, width, 2, TILE, lanes), f32),
            pltpu.VMEM((rows, 2, TILE, lanes), f32),
            pltpu.VMEM((rows, 2, TILE, lanes), f32),
            pltpu.VMEM((rows, 2, TILE, lanes), f32),
            dma((2, 3)),
            dma((2, 3)),
            dma((2, 3)),
            dma((2, 5)),
            dma((2, rounds, 2, tiles)),
            dma((2, tiles)),
        ],
        compiler_params=pltpu.CompilerParams(
            collective_id=0, has_side_effects=True, vmem_limit_bytes=32 * 1024 * 1024
        ),
        cost_estimate=pl.CostEstimate(flops=60_000_000, bytes_accessed=4_000_000, transcendentals=0),
    )(masked, wet, vert_corr, kappa)
    return result.transpose(0, 1, 3, 2, 4).reshape(increments.shape)


def fits(mesh):
    shape = mesh.shape
    return shape["lev"] == 2 and shape["gy"] == 2 and shape["gx"] > 2


def solution(mesh):
    in_specs = (
        P(None, None, "lev", "gx", "gy"),
        P(),
        P(None, "gx", "gy"),
        P("lev", "gx", "gy"),
        P("gx", "gy"),
    )
    out_specs = P(None, None, "lev", "gx", "gy")
    return jax.shard_map(
        fused if fits(mesh) else per_device, mesh=mesh, in_specs=in_specs, out_specs=out_specs, check_vma=False
    )
```

```python
import jax
import jax.numpy as jnp
from jax import lax
from jax.experimental import pallas as pl
from jax.experimental.pallas import tpu as pltpu
from jax.sharding import PartitionSpec as P

PASSES = 10


def from_behind(block, axis, distance):
    devices = range(lax.axis_size(axis))
    route = [((i - distance) % len(devices), i) for i in devices]
    return lax.ppermute(block, axis, route)


def shifted(block, axis, distance):
    devices = range(lax.axis_size(axis))
    route = [(i - distance, i) for i in devices if i - distance in devices]
    return lax.ppermute(block, axis, route)


def padded(cells, sides, width):
    for axis, dim in sides:
        count = lax.axis_size(axis)
        head = lax.slice_in_dim(cells, 0, width, axis=dim)
        tail = lax.slice_in_dim(cells, cells.shape[dim] - width, cells.shape[dim], axis=dim)
        cells = jnp.concatenate(
            [
                lax.ppermute(tail, axis, [(i, (i + 1) % count) for i in range(count)]),
                cells,
                lax.ppermute(head, axis, [((i + 1) % count, i) for i in range(count)]),
            ],
            axis=dim,
        )
    return cells


def relax(extended, east_ext, north_ext, wet_center):
    center = extended[..., 1:-1, 1:-1]
    flux = east_ext[1:-1, 1:-1] * (extended[..., 2:, 1:-1] - center)
    flux = flux + east_ext[:-2, 1:-1] * (extended[..., :-2, 1:-1] - center)
    flux = flux + north_ext[1:-1, 1:-1] * (extended[..., 1:-1, 2:] - center)
    flux = flux + north_ext[1:-1, :-2] * (extended[..., 1:-1, :-2] - center)
    return wet_center * (center + flux)


def per_device(increments, vert_corr, kappa, sea_mask, level_count):
    lev_dev = sea_mask.shape[0]
    cells_x = sea_mask.shape[1]
    cells_y = sea_mask.shape[2]
    lev_first = lax.axis_index("lev") * lev_dev
    levels = lev_first + jnp.arange(lev_dev, dtype=jnp.int32)
    wet = sea_mask * (levels[:, None, None] < level_count[None]).astype(jnp.int32)
    wet_float = wet.astype(jnp.float32)
    masked = increments * wet_float
    own_rows = lax.dynamic_slice_in_dim(vert_corr, lev_first, lev_dev, 1)
    correlated = jnp.einsum(
        "toh,dthxy->dtoxy",
        own_rows,
        lax.all_gather(masked, "lev", axis=2, tiled=True),
        precision=lax.Precision.HIGHEST,
    )
    field = correlated * wet_float
    total_y = cells_y * lax.axis_size("gy")
    local_rows = lax.axis_index("gy") * cells_y + jnp.arange(cells_y, dtype=jnp.int32)
    open_local = (local_rows != total_y - 1).astype(jnp.float32)
    east_local = kappa[0]
    north_local = kappa[1] * open_local[None, :]
    east_low = from_behind(east_local[-1:, :], "gx", 1)
    north_low = shifted(north_local[:, -1:], "gy", 1)
    zero_row = jnp.zeros((1, cells_y), jnp.float32)
    zero_col = jnp.zeros((cells_x, 1), jnp.float32)
    east_ext = jnp.pad(jnp.concatenate([east_low, east_local, zero_row], axis=0), ((0, 0), (1, 1)))
    north_ext = jnp.pad(
        jnp.concatenate([north_low, north_local, zero_col], axis=1), ((1, 1), (0, 0))
    )

    def one_pass(step, current):
        extended = padded(current, (("gx", 3), ("gy", 4)), 1)
        return relax(extended, east_ext, north_ext, wet_float)

    field = lax.fori_loop(0, PASSES, one_pass, field)
    return field


TILE = 8
LANES = 128
FULL = 4
HALO = PASSES
MESH = pl.DeviceIdType.MESH


def remote(src, dst, send_sem, recv_sem, device):
    return pltpu.make_async_remote_copy(
        src_ref=src,
        dst_ref=dst,
        send_sem=send_sem,
        recv_sem=recv_sem,
        device_id=device,
        device_id_type=MESH,
    )


def kernel(
    inc_ref, corr_ref, kappa_ref, sea_ref, count_ref, out_ref,
    wsrc, psum, xrecv, field, last, wet, wet_last, kap, east, north, south, stage, stage_last,
    x_sems, y_sems, z_sems, last_sems, wet_sems, kap_sems, out_sems,
):
    lev, gx, gy = lax.axis_index("lev"), lax.axis_index("gx"), lax.axis_index("gy")
    count = lax.axis_size("gx")
    y = lax.rem(gx, 2)
    cells = kappa_ref.shape[1]
    levels = sea_ref.shape[0] // cells
    rows = 2 * cells + 2 * HALO
    rows_last = cells + 2 * HALO
    own_start = HALO + cells * y

    pair = {"lev": 1 - lev}
    mate = {"gy": 1 - gy}
    over = {"gx": gx + 1 - 2 * y}
    cross = {"gx": gx + 1 - 2 * y, "gy": 1 - gy}
    z_east = {"gx": lax.rem(gx + 2, count)}
    z_west = {"gx": lax.rem(gx + count - 2, count)}
    east_dev = {"gx": lax.rem(gx + 1, count)}
    west_dev = {"gx": lax.rem(gx + count - 1, count)}
    outer = {"gx": lax.rem(gx + count - 1 + 2 * y, count)}
    z_early = {"gx": lax.rem(gx + count + 2 - 4 * y, count)}
    z_late = {"gx": lax.rem(gx + count - 2 + 4 * y, count)}
    k_own = 2 * y + gy
    k_mate = 2 * y + 1 - gy
    k_over = 2 * (1 - y) + gy
    k_cross = 2 * (1 - y) + 1 - gy
    order = (FULL, k_over, k_cross, k_mate, k_own)

    barrier = pltpu.get_barrier_semaphore()
    everyone = (pair, mate, over, cross, z_east, z_west, outer)
    for device in everyone:
        pl.semaphore_signal(barrier, inc=1, device_id=device, device_id_type=MESH)

    number = lev * levels + lax.broadcasted_iota(jnp.int32, (levels, LANES), 0)
    for x in range(cells):
        sea = sea_ref[pl.ds(x, levels, stride=cells), :]
        value = jnp.where(number < count_ref[x:x + 1, :], sea, 0).astype(jnp.float32)
        for k in range(FULL + 1):
            wsrc[k, x] = value[k * TILE:(k + 1) * TILE]
    columns = gy * LANES + lax.broadcasted_iota(jnp.int32, (1, LANES), 1)
    is_open = (columns != LANES * lax.axis_size("gy") - 1).astype(jnp.float32)
    kap[1 + y, gy, 0] = kappa_ref[0]
    kap[1 + y, gy, 1] = kappa_ref[1] * is_open
    wet[gy, pl.ds(own_start, cells)] = wsrc[k_own]
    wet_last[gy, HALO:HALO + cells] = wsrc[FULL]

    def vertical(t):
        whole = corr_ref[t]
        corr = jnp.where(lev == 0, whole[:, :levels], whole[:, levels:])
        high = corr.astype(jnp.bfloat16).astype(jnp.float32)
        weights = jnp.concatenate([high, high, corr - high], axis=1).astype(jnp.bfloat16)
        for x in range(0, cells, 2):
            sides = []
            for p in range(2):
                here = jnp.concatenate([wsrc[k, x + p] for k in range(FULL + 1)], axis=0)
                sides.append(inc_ref[t, pl.ds(x + p, levels, stride=cells), :] * here)
            both = jnp.concatenate(sides, axis=1)
            top = both.astype(jnp.bfloat16).astype(jnp.float32)
            stack = jnp.concatenate([top, both - top, top], axis=0).astype(jnp.bfloat16)
            result = jnp.dot(weights, stack, preferred_element_type=jnp.float32)
            for side in range(2):
                for k in range(FULL + 1):
                    at = side * levels + k * TILE
                    for p in range(2):
                        psum[side, t, k, x + p] = result[at:at + TILE, p * LANES:(p + 1) * LANES]

    x_copies = [
        [remote(psum.at[1 - lev, t, k], xrecv.at[t, k], x_sems.at[0, t, n], x_sems.at[1, t, n], pair)
         for n, k in enumerate(order)]
        for t in range(2)
    ]
    vertical(0)
    pl.semaphore_wait(barrier, len(everyone))
    for copy in x_copies[0]:
        copy.start()

    span = pl.ds(own_start, cells)
    mine = kap.at[1 + y, gy]
    kap_copies = [
        remote(mine, mine, kap_sems.at[0, n], kap_sems.at[1, n], device)
        for n, device in enumerate((mate, over, cross))
    ]
    wet_copies = [
        remote(wsrc.at[k], wet.at[gy, span], wet_sems.at[0, n], wet_sems.at[1, n], device)
        for n, (k, device) in enumerate(((k_mate, mate), (k_over, over), (k_cross, cross)))
    ]
    wet_copies.append(remote(
        wsrc.at[FULL], wet_last.at[gy, pl.ds(HALO, cells)], wet_sems.at[0, 3], wet_sems.at[1, 3], mate))
    for copy in kap_copies + wet_copies:
        copy.start()
    vertical(1)
    for copy in x_copies[1]:
        copy.start()

    for copy in kap_copies:
        copy.wait()
    kap_far = [
        remote(kap.at[1], kap.at[3], kap_sems.at[0, 3], kap_sems.at[1, 3], z_west),
        remote(kap.at[2], kap.at[0], kap_sems.at[0, 4], kap_sems.at[1, 4], z_east),
    ]
    for copy in kap_far:
        copy.start()
    wet_copies[3].wait()

    def ring(buffer, sems, first):
        return [
            remote(buffer.at[:, pl.ds(HALO, HALO)], buffer.at[:, pl.ds(HALO + cells, HALO)],
                   sems.at[0, first], sems.at[1, first], west_dev),
            remote(buffer.at[:, pl.ds(cells, HALO)], buffer.at[:, pl.ds(0, HALO)],
                   sems.at[0, first + 1], sems.at[1, first + 1], east_dev),
        ]

    wet_ring = ring(wet_last, wet_sems, 4)
    for copy in wet_ring:
        copy.start()
    for copy in wet_copies[:3]:
        copy.wait()
    wet_far = [
        remote(wet.at[:, pl.ds(HALO, HALO)], wet.at[:, pl.ds(rows - HALO, HALO)],
               wet_sems.at[0, 6], wet_sems.at[1, 6], z_west),
        remote(wet.at[:, pl.ds(2 * cells, HALO)], wet.at[:, pl.ds(0, HALO)],
               wet_sems.at[0, 7], wet_sems.at[1, 7], z_east),
    ]
    for copy in wet_far:
        copy.start()

    def finish(t, n):
        x_copies[t][n].wait_recv()
        k = order[n]
        value = wsrc[k] * (psum[lev, t, k] + xrecv[t, k])
        psum[lev, t, k] = value
        return value

    last_copy = remote(
        psum.at[lev, 1 - gy, FULL], last.at[gy, pl.ds(HALO, cells)],
        last_sems.at[0, 0], last_sems.at[1, 0], mate)
    y_copies = [
        [remote(psum.at[lev, t, k], field.at[t, gy, span], y_sems.at[0, t, n], y_sems.at[1, t, n], device)
         for n, (k, device) in enumerate(((k_over, over), (k_cross, cross), (k_mate, mate)))]
        for t in range(2)
    ]
    low, high_row = 2 * cells - (2 * cells - HALO) * y, HALO + (2 * cells - HALO) * y
    z_copies = [
        [remote(field.at[t, :, pl.ds(low, HALO)], field.at[t, :, pl.ds((rows - HALO) * y, HALO)],
                z_sems.at[0, t, 0], z_sems.at[1, t, 0], z_early),
         remote(field.at[t, :, pl.ds(high_row, HALO)], field.at[t, :, pl.ds((rows - HALO) * (1 - y), HALO)],
                z_sems.at[0, t, 1], z_sems.at[1, t, 1], z_late)]
        for t in range(2)
    ]

    def take_last(t):
        value = finish(t, 0)

        @pl.when(gy == t)
        def _():
            last[gy, HALO:HALO + cells] = value

        @pl.when(gy != t)
        def _():
            last_copy.start()

    def hand_over(t, n):
        finish(t, n)
        y_copies[t][n - 1].start()

    def keep(t):
        field[t, gy, span] = finish(t, 4)
        y_copies[t][2].wait_recv()
        z_copies[t][1].start()

    def early(t):
        y_copies[t][0].wait_recv()
        y_copies[t][1].wait_recv()
        z_copies[t][0].start()

    lane = lax.broadcasted_iota(jnp.int32, (TILE, LANES), 1)
    at_end = lane == LANES - 1
    at_start = lane == 0

    def coefficients():
        for row in range(rows):
            block, place = divmod(row + cells - HALO, cells)
            moved = []
            for h in range(2):
                east[row, h] = jnp.broadcast_to(kap[block, h, 0, place:place + 1], (TILE, LANES))
                value = jnp.broadcast_to(kap[block, h, 1, place:place + 1], (TILE, LANES))
                north[row, h] = value
                moved.append(pltpu.roll(value, 1, 1))
            south[row, 0] = jnp.where(at_start, moved[1], moved[0])
            south[row, 1] = jnp.where(at_start, moved[0], moved[1])

    def relax(cells_ref, wet_ref, height, base, put):
        for step in range(HALO):
            first, final = step + 1, height - 2 - step
            before = [cells_ref[h, first - 1] for h in range(2)]
            here = [cells_ref[h, first] for h in range(2)]
            flux = [east[base + first - 1, h] * (here[h] - before[h]) for h in range(2)]
            for row in range(first, final + 1):
                after = [cells_ref[h, row + 1] for h in range(2)]
                turned = [pltpu.roll(here[h], LANES - 1, 1) for h in range(2)]
                back = [pltpu.roll(here[h], 1, 1) for h in range(2)]
                up = [jnp.where(at_end, turned[1], turned[0]), turned[1]]
                down = [back[0], jnp.where(at_start, back[0], back[1])]
                ahead = [east[base + row, h] * (after[h] - here[h]) for h in range(2)]
                for h in range(2):
                    rise = north[base + row, h] * (up[h] - here[h])
                    fall = south[base + row, h] * (here[h] - down[h])
                    total = wet_ref[h, row] * (here[h] + ((ahead[h] - flux[h]) + (rise - fall)))
                    if step == HALO - 1:
                        put(row - HALO, h, total)
                    else:
                        cells_ref[h, row] = total
                here, flux = after, ahead

    def relax_full(t):
        def put(row, h, value):
            part, place = divmod(row, cells)
            stage[t, part, h, pl.ds(place, TILE, stride=cells), :] = value

        relax(field.at[t], wet, rows, 0, put)

    def relax_last():
        def put(row, h, value):
            stage_last[h, pl.ds(row, TILE, stride=cells), :] = value

        relax(last, wet_last, rows_last, cells * y, put)

    out_copies = [
        [remote(stage.at[t, part, half], out_ref.at[t, k_own], out_sems.at[0, t, n], out_sems.at[1, t, n], device)
         for n, (part, half, device) in enumerate(
             ((1 - y, gy, over), (1 - y, 1 - gy, cross), (y, 1 - gy, mate)))]
        for t in range(2)
    ]
    last_out = remote(stage_last.at[1 - gy], out_ref.at[gy, FULL], last_sems.at[0, 3], last_sems.at[1, 3], mate)

    def deliver(t):
        for copy in out_copies[t]:
            copy.start()
        out_ref[t, k_own] = stage[t, y, gy]

    take_last(0)
    hand_over(0, 1)
    hand_over(0, 2)
    hand_over(0, 3)
    early(0)
    for copy in kap_far:
        copy.wait()
    coefficients()
    keep(0)
    take_last(1)
    hand_over(1, 1)
    last_copy.wait_recv()
    last_ring = ring(last, last_sems, 1)
    for copy in last_ring:
        copy.start()
    for copy in wet_far + wet_ring:
        copy.wait()
    for copy in z_copies[0]:
        copy.wait()
    relax_full(0)
    deliver(0)
    hand_over(1, 2)
    hand_over(1, 3)
    early(1)
    keep(1)
    for copy in last_ring:
        copy.wait()
    relax_last()
    last_out.start()
    out_ref[gy, FULL] = stage_last[gy]
    for copy in z_copies[1]:
        copy.wait()
    relax_full(1)
    deliver(1)

    last_copy.wait_send()
    for t in range(2):
        for copy in x_copies[t] + y_copies[t]:
            copy.wait_send()
    for copy in out_copies[0] + out_copies[1] + [last_out]:
        copy.wait()


def fused(increments, vert_corr, kappa, sea_mask, level_count):
    levels, cells, lanes = sea_mask.shape
    if levels != (FULL + 1) * TILE or cells < HALO or cells % TILE or lanes != LANES:
        return per_device(increments, vert_corr, kappa, sea_mask, level_count)
    tiles = FULL + 1
    rows = 2 * cells + 2 * HALO
    rows_last = cells + 2 * HALO
    vmem = pl.BlockSpec(memory_space=pltpu.VMEM)
    f32 = jnp.float32
    dma = pltpu.SemaphoreType.DMA
    result = pl.pallas_call(
        kernel,
        out_shape=jax.ShapeDtypeStruct((2, tiles, TILE * cells, lanes), f32),
        in_specs=[vmem] * 5,
        out_specs=vmem,
        scratch_shapes=[
            pltpu.VMEM((tiles, cells, TILE, lanes), f32),
            pltpu.VMEM((2, 2, tiles, cells, TILE, lanes), f32),
            pltpu.VMEM((2, tiles, cells, TILE, lanes), f32),
            pltpu.VMEM((2, 2, rows, TILE, lanes), f32),
            pltpu.VMEM((2, rows_last, TILE, lanes), f32),
            pltpu.VMEM((2, rows, TILE, lanes), f32),
            pltpu.VMEM((2, rows_last, TILE, lanes), f32),
            pltpu.VMEM((4, 2, 2, cells, lanes), f32),
            pltpu.VMEM((rows, 2, TILE, lanes), f32),
            pltpu.VMEM((rows, 2, TILE, lanes), f32),
            pltpu.VMEM((rows, 2, TILE, lanes), f32),
            pltpu.VMEM((2, 2, 2, TILE * cells, lanes), f32),
            pltpu.VMEM((2, TILE * cells, lanes), f32),
            dma((2, 2, tiles)),
            dma((2, 2, 3)),
            dma((2, 2, 2)),
            dma((2, 4)),
            dma((2, 8)),
            dma((2, 5)),
            dma((2, 2, 3)),
        ],
        compiler_params=pltpu.CompilerParams(
            collective_id=0, has_side_effects=True, vmem_limit_bytes=32 * 1024 * 1024
        ),
        cost_estimate=pl.CostEstimate(flops=60_000_000, bytes_accessed=4_000_000, transcendentals=0),
    )(
        increments.reshape(2, levels * cells, lanes), vert_corr, kappa,
        sea_mask.reshape(levels * cells, lanes), level_count,
    )
    return result.reshape(increments.shape)


def fits(mesh):
    shape = mesh.shape
    return shape["lev"] == 2 and shape["gy"] == 2 and shape["gx"] > 4 and shape["gx"] % 2 == 0


def solution(mesh):
    in_specs = (
        P(None, None, "lev", "gx", "gy"),
        P(),
        P(None, "gx", "gy"),
        P("lev", "gx", "gy"),
        P("gx", "gy"),
    )
    out_specs = P(None, None, "lev", "gx", "gy")
    return jax.shard_map(
        fused if fits(mesh) else per_device, mesh=mesh, in_specs=in_specs, out_specs=out_specs, check_vma=False
    )
```

```python
import jax
import jax.numpy as jnp
from jax import lax
from jax.experimental import pallas as pl
from jax.experimental.pallas import tpu as pltpu
from jax.sharding import PartitionSpec as P

PASSES = 10


def from_behind(block, axis, distance):
    devices = range(lax.axis_size(axis))
    route = [((i - distance) % len(devices), i) for i in devices]
    return lax.ppermute(block, axis, route)


def shifted(block, axis, distance):
    devices = range(lax.axis_size(axis))
    route = [(i - distance, i) for i in devices if i - distance in devices]
    return lax.ppermute(block, axis, route)


def padded(cells, sides, width):
    for axis, dim in sides:
        count = lax.axis_size(axis)
        head = lax.slice_in_dim(cells, 0, width, axis=dim)
        tail = lax.slice_in_dim(cells, cells.shape[dim] - width, cells.shape[dim], axis=dim)
        cells = jnp.concatenate(
            [
                lax.ppermute(tail, axis, [(i, (i + 1) % count) for i in range(count)]),
                cells,
                lax.ppermute(head, axis, [((i + 1) % count, i) for i in range(count)]),
            ],
            axis=dim,
        )
    return cells


def relax(extended, east_ext, north_ext, wet_center):
    center = extended[..., 1:-1, 1:-1]
    flux = east_ext[1:-1, 1:-1] * (extended[..., 2:, 1:-1] - center)
    flux = flux + east_ext[:-2, 1:-1] * (extended[..., :-2, 1:-1] - center)
    flux = flux + north_ext[1:-1, 1:-1] * (extended[..., 1:-1, 2:] - center)
    flux = flux + north_ext[1:-1, :-2] * (extended[..., 1:-1, :-2] - center)
    return wet_center * (center + flux)


def per_device(increments, vert_corr, kappa, sea_mask, level_count):
    lev_dev = sea_mask.shape[0]
    cells_x = sea_mask.shape[1]
    cells_y = sea_mask.shape[2]
    lev_first = lax.axis_index("lev") * lev_dev
    levels = lev_first + jnp.arange(lev_dev, dtype=jnp.int32)
    wet = sea_mask * (levels[:, None, None] < level_count[None]).astype(jnp.int32)
    wet_float = wet.astype(jnp.float32)
    masked = increments * wet_float
    own_rows = lax.dynamic_slice_in_dim(vert_corr, lev_first, lev_dev, 1)
    correlated = jnp.einsum(
        "toh,dthxy->dtoxy",
        own_rows,
        lax.all_gather(masked, "lev", axis=2, tiled=True),
        precision=lax.Precision.HIGHEST,
    )
    field = correlated * wet_float
    total_y = cells_y * lax.axis_size("gy")
    local_rows = lax.axis_index("gy") * cells_y + jnp.arange(cells_y, dtype=jnp.int32)
    open_local = (local_rows != total_y - 1).astype(jnp.float32)
    east_local = kappa[0]
    north_local = kappa[1] * open_local[None, :]
    east_low = from_behind(east_local[-1:, :], "gx", 1)
    north_low = shifted(north_local[:, -1:], "gy", 1)
    zero_row = jnp.zeros((1, cells_y), jnp.float32)
    zero_col = jnp.zeros((cells_x, 1), jnp.float32)
    east_ext = jnp.pad(jnp.concatenate([east_low, east_local, zero_row], axis=0), ((0, 0), (1, 1)))
    north_ext = jnp.pad(
        jnp.concatenate([north_low, north_local, zero_col], axis=1), ((1, 1), (0, 0))
    )

    def one_pass(step, current):
        extended = padded(current, (("gx", 3), ("gy", 4)), 1)
        return relax(extended, east_ext, north_ext, wet_float)

    field = lax.fori_loop(0, PASSES, one_pass, field)
    return field


TILE = 8
LANES = 128
WIDTH = 5
MESH = pl.DeviceIdType.MESH


def remote(src, dst, send_sem, recv_sem, device):
    return pltpu.make_async_remote_copy(
        src_ref=src,
        dst_ref=dst,
        send_sem=send_sem,
        recv_sem=recv_sem,
        device_id=device,
        device_id_type=MESH,
    )


def kernel(
    inc_hbm, corr_hbm, kappa_hbm, sea_hbm, count_hbm, out_ref,
    inc_ref, corr_ref, kappa_ref, sea_ref, count_ref, masked_ref,
    geo, own, other, field, halo, east, north, south,
    own_sems, same_sems, cross_sems, geo_sems, halo_sems, out_sems, in_sems, keep_sems,
):
    lev, gx, gy = lax.axis_index("lev"), lax.axis_index("gx"), lax.axis_index("gy")
    count = lax.axis_size("gx")
    cells = masked_ref.shape[1]
    levels = masked_ref.shape[2]
    lanes = masked_ref.shape[3]
    tiles = levels // TILE
    width = WIDTH
    rows = cells + 2 * width
    rounds = PASSES // width
    east_dev = {"gx": lax.rem(gx + 1, count)}
    west_dev = {"gx": lax.rem(gx + count - 1, count)}
    mate = {"gy": 1 - gy}
    pair = {"lev": 1 - lev}
    cross = {"lev": 1 - lev, "gy": 1 - gy}

    loads = [
        pltpu.make_async_copy(src, dst, in_sems.at[n])
        for n, (src, dst) in enumerate((
            (sea_hbm, sea_ref), (count_hbm, count_ref), (kappa_hbm, kappa_ref),
            (inc_hbm, inc_ref), (corr_hbm, corr_ref)))
    ]
    for load in loads:
        load.start()
    barrier = pltpu.get_barrier_semaphore()
    everyone = (east_dev, west_dev, mate, pair, cross)
    for device in everyone:
        pl.semaphore_signal(barrier, inc=1, device_id=device, device_id_type=MESH)
    columns = gy * lanes + lax.broadcasted_iota(jnp.int32, (1, lanes), 1)
    is_open = (columns != lanes * lax.axis_size("gy") - 1).astype(jnp.float32)
    for load in loads:
        load.wait()
    number = lev * levels + lax.broadcasted_iota(jnp.int32, (levels, lanes), 0)
    for x in range(cells):
        sea = sea_ref[pl.ds(x, levels, stride=cells), :]
        value = jnp.where(number < count_ref[x:x + 1, :], sea, 0).astype(jnp.float32)
        geo[gy, width + x, 0:levels] = value
        for t in range(2):
            masked_ref[t, x] = inc_ref[t, pl.ds(x, levels, stride=cells), :] * value
        geo[gy, width + x, levels:levels + 1] = kappa_ref[0, x:x + 1]
        geo[gy, width + x, levels + 1:levels + 2] = kappa_ref[1, x:x + 1] * is_open
        geo[gy, width + x, levels + 2:] = jnp.zeros((TILE - 2, lanes), jnp.float32)
    pl.semaphore_wait(barrier, len(everyone))

    starts = ((0, width), (cells - width, width), (width, cells - 2 * width))
    own_copies, same_copies, cross_copies = [], [], []
    for q, (start, size) in enumerate(starts):
        span = pl.ds(start, size)
        own_copies.append(remote(
            masked_ref.at[1 - gy, span], own.at[span], own_sems.at[0, q], own_sems.at[1, q], mate))
        same_copies.append(remote(
            masked_ref.at[gy, span], other.at[gy, span],
            same_sems.at[0, q], same_sems.at[1, q], pair))
        cross_copies.append(remote(
            masked_ref.at[1 - gy, span], other.at[gy, span],
            cross_sems.at[0, q], cross_sems.at[1, q], cross))
    geo_copies = [
        remote(geo.at[gy, pl.ds(width, cells)], geo.at[gy, pl.ds(width, cells)], geo_sems.at[0, 0], geo_sems.at[1, 0], mate),
        remote(geo.at[gy, pl.ds(cells, width)],
               geo.at[gy, pl.ds(0, width)],
               geo_sems.at[0, 1], geo_sems.at[1, 1], east_dev),
        remote(geo.at[gy, pl.ds(width, width)],
               geo.at[gy, pl.ds(width + cells, width)],
               geo_sems.at[0, 2], geo_sems.at[1, 2], west_dev),
    ]
    for q in range(len(starts)):
        same_copies[q].start()
        cross_copies[q].start()
        if q == 0:
            for copy in geo_copies[1:]:
                copy.start()
            geo_copies[0].start()
        own_copies[q].start()

    mine = corr_ref[gy, pl.ds(pl.multiple_of(lev * levels, TILE), levels), :]
    swapped = jnp.concatenate([mine[:, levels:], mine[:, :levels]], axis=1)
    corr = jnp.where(lev == 0, mine, swapped)
    high = corr.astype(jnp.bfloat16)
    low = (corr - high.astype(jnp.float32)).astype(jnp.bfloat16)
    weights = jnp.concatenate([high, high, low], axis=1)

    def halo_copies(r, k):
        return (
            remote(field.at[k, pl.ds(width, width)], halo.at[r, 1, k],
                   halo_sems.at[0, r, 0, k], halo_sems.at[1, r, 0, k], west_dev),
            remote(field.at[k, pl.ds(cells, width)], halo.at[r, 0, k],
                   halo_sems.at[0, r, 1, k], halo_sems.at[1, r, 1, k], east_dev),
        )

    def vertical(x):
        mine = masked_ref[gy, x]
        theirs = own[x]
        first = jnp.where(gy == 0, mine, theirs)
        second = jnp.where(gy == 0, theirs, mine)
        near = jnp.concatenate([first, second], axis=1)
        far = jnp.concatenate([other[0, x], other[1, x]], axis=1)
        both = jnp.concatenate([near, far], axis=0)
        top = both.astype(jnp.bfloat16)
        rest = (both - top.astype(jnp.float32)).astype(jnp.bfloat16)
        stack = jnp.concatenate([top, rest, top], axis=0)
        result = jnp.dot(weights, stack, preferred_element_type=jnp.float32)
        for half in range(2):
            for k in range(tiles):
                value = result[k * TILE:(k + 1) * TILE, half * LANES:(half + 1) * LANES]
                wet = geo[half, width + x, k * TILE:(k + 1) * TILE]
                field[k, width + x, half] = value * wet

    pending = [halo_copies(0, k) for k in range(tiles)]
    forward = []
    geo_copies[0].wait()
    for q, (start, size) in enumerate(starts):
        own_copies[q].wait()
        same_copies[q].wait()
        cross_copies[q].wait()
        for x in range(start, start + size):
            vertical(x)
        if q < 2:
            for k in range(tiles):
                pending[k][q].start()
        if q == 1:
            for side, place in ((1, 0), (2, width + cells)):
                geo_copies[side].wait()
                edge = geo.at[gy, pl.ds(place, width)]
                forward.append(remote(
                    edge, edge, geo_sems.at[0, 2 + side], geo_sems.at[1, 2 + side], mate))
                forward[-1].start()
    for copy in forward:
        copy.wait()
    for half in range(2):
        for row in range(rows):
            east[row, half] = jnp.broadcast_to(geo[half, row, levels:levels + 1], (TILE, LANES))
            north[row, half] = jnp.broadcast_to(geo[half, row, levels + 1:levels + 2], (TILE, LANES))

    lane = lax.broadcasted_iota(jnp.int32, (TILE, LANES), 1)
    at_end = lane == LANES - 1
    at_start = lane == 0
    for row in range(rows):
        moved = [pltpu.roll(north[row, h], 1, 1) for h in range(2)]
        south[row, 0] = jnp.where(at_start, moved[1], moved[0])
        south[row, 1] = jnp.where(at_start, moved[0], moved[1])

    def relax_tile(r, k):
        for step in range(width):
            def row_of(row):
                if step == 0 and row < width:
                    return halo[r, 0, k, row, 0], halo[r, 0, k, row, 1]
                if step == 0 and row >= width + cells:
                    at = row - width - cells
                    return halo[r, 1, k, at, 0], halo[r, 1, k, at, 1]
                return field[k, row, 0], field[k, row, 1]

            first, last = step + 1, rows - 2 - step
            before, here = row_of(first - 1), row_of(first)
            flux = [east[first - 1, h] * (here[h] - before[h]) for h in range(2)]
            for row in range(first, last + 1):
                after = row_of(row + 1)
                turned = [pltpu.roll(here[h], LANES - 1, 1) for h in range(2)]
                up = [jnp.where(at_end, turned[1], turned[0]), turned[1]]
                back = [pltpu.roll(here[h], 1, 1) for h in range(2)]
                below = [back[0], jnp.where(at_start, back[0], back[1])]
                rise = [north[row, h] * (up[h] - here[h]) for h in range(2)]
                down = [south[row, h] * (here[h] - below[h]) for h in range(2)]
                ahead = [east[row, h] * (after[h] - here[h]) for h in range(2)]
                for h in range(2):
                    wet = geo[h, row, k * TILE:(k + 1) * TILE]
                    total = here[h] + ((ahead[h] - flux[h]) + (rise[h] - down[h]))
                    field[k, row, h] = wet * total
                here, flux = after, ahead

    out_copies = []
    for r in range(rounds):
        later = []
        for k in range(tiles):
            for copy in pending[k]:
                copy.wait()
            relax_tile(r, k)
            if r < rounds - 1:
                later.append(halo_copies(r + 1, k))
                for copy in later[-1]:
                    copy.start()
            else:
                out_copies.append(remote(
                    field.at[k, pl.ds(width, cells), 1 - gy], out_ref.at[gy, k],
                    out_sems.at[0, k], out_sems.at[1, k], mate))
                out_copies[-1].start()
                out_copies.append(pltpu.make_async_copy(
                    field.at[k, pl.ds(width, cells), gy], out_ref.at[gy, k], keep_sems.at[k]))
                out_copies[-1].start()
        pending = later
    for copy in out_copies:
        copy.wait()


def fused(increments, vert_corr, kappa, sea_mask, level_count):
    levels, cells, lanes = sea_mask.shape
    tiles = levels // TILE
    width = WIDTH
    rows = cells + 2 * width
    rounds = PASSES // width
    hbm = pl.BlockSpec(memory_space=pl.ANY)
    f32 = jnp.float32
    dma = pltpu.SemaphoreType.DMA
    result = pl.pallas_call(
        kernel,
        out_shape=jax.ShapeDtypeStruct((2, tiles, cells, TILE, lanes), f32),
        in_specs=[hbm] * 5,
        out_specs=hbm,
        scratch_shapes=[
            pltpu.VMEM((2, levels * cells, lanes), f32),
            pltpu.VMEM(vert_corr.shape, f32),
            pltpu.VMEM(kappa.shape, f32),
            pltpu.VMEM((levels * cells, lanes), sea_mask.dtype),
            pltpu.VMEM(level_count.shape, level_count.dtype),
            pltpu.VMEM((2, cells, levels, lanes), f32),
            pltpu.VMEM((2, rows, levels + TILE, lanes), f32),
            pltpu.VMEM((cells, levels, lanes), f32),
            pltpu.VMEM((2, cells, levels, lanes), f32),
            pltpu.VMEM((tiles, rows, 2, TILE, lanes), f32),
            pltpu.VMEM((rounds, 2, tiles, width, 2, TILE, lanes), f32),
            pltpu.VMEM((rows, 2, TILE, lanes), f32),
            pltpu.VMEM((rows, 2, TILE, lanes), f32),
            pltpu.VMEM((rows, 2, TILE, lanes), f32),
            dma((2, 3)),
            dma((2, 3)),
            dma((2, 3)),
            dma((2, 5)),
            dma((2, rounds, 2, tiles)),
            dma((2, tiles)),
            dma((5,)),
            dma((tiles,)),
        ],
        compiler_params=pltpu.CompilerParams(
            collective_id=0, has_side_effects=True, vmem_limit_bytes=58 * 1024 * 1024
        ),
        cost_estimate=pl.CostEstimate(flops=60_000_000, bytes_accessed=4_000_000, transcendentals=0),
    )(
        increments.reshape(2, levels * cells, lanes), vert_corr, kappa,
        sea_mask.reshape(levels * cells, lanes), level_count,
    )
    return result.transpose(0, 1, 3, 2, 4).reshape(increments.shape)


def fits(mesh):
    shape = mesh.shape
    return shape["lev"] == 2 and shape["gy"] == 2 and shape["gx"] > 2


def solution(mesh):
    in_specs = (
        P(None, None, "lev", "gx", "gy"),
        P(),
        P(None, "gx", "gy"),
        P("lev", "gx", "gy"),
        P("gx", "gy"),
    )
    out_specs = P(None, None, "lev", "gx", "gy")
    return jax.shard_map(
        fused if fits(mesh) else per_device, mesh=mesh, in_specs=in_specs, out_specs=out_specs, check_vma=False
    )
```

```python
import jax
import jax.numpy as jnp
from jax import lax
from jax.experimental import pallas as pl
from jax.experimental.pallas import tpu as pltpu
from jax.sharding import PartitionSpec as P

PASSES = 10


def from_behind(block, axis, distance):
    devices = range(lax.axis_size(axis))
    route = [((i - distance) % len(devices), i) for i in devices]
    return lax.ppermute(block, axis, route)


def shifted(block, axis, distance):
    devices = range(lax.axis_size(axis))
    route = [(i - distance, i) for i in devices if i - distance in devices]
    return lax.ppermute(block, axis, route)


def padded(cells, sides, width):
    for axis, dim in sides:
        count = lax.axis_size(axis)
        head = lax.slice_in_dim(cells, 0, width, axis=dim)
        tail = lax.slice_in_dim(cells, cells.shape[dim] - width, cells.shape[dim], axis=dim)
        cells = jnp.concatenate(
            [
                lax.ppermute(tail, axis, [(i, (i + 1) % count) for i in range(count)]),
                cells,
                lax.ppermute(head, axis, [((i + 1) % count, i) for i in range(count)]),
            ],
            axis=dim,
        )
    return cells


def relax(extended, east_ext, north_ext, wet_center):
    center = extended[..., 1:-1, 1:-1]
    flux = east_ext[1:-1, 1:-1] * (extended[..., 2:, 1:-1] - center)
    flux = flux + east_ext[:-2, 1:-1] * (extended[..., :-2, 1:-1] - center)
    flux = flux + north_ext[1:-1, 1:-1] * (extended[..., 1:-1, 2:] - center)
    flux = flux + north_ext[1:-1, :-2] * (extended[..., 1:-1, :-2] - center)
    return wet_center * (center + flux)


def per_device(increments, vert_corr, kappa, sea_mask, level_count):
    lev_dev = sea_mask.shape[0]
    cells_x = sea_mask.shape[1]
    cells_y = sea_mask.shape[2]
    lev_first = lax.axis_index("lev") * lev_dev
    levels = lev_first + jnp.arange(lev_dev, dtype=jnp.int32)
    wet = sea_mask * (levels[:, None, None] < level_count[None]).astype(jnp.int32)
    wet_float = wet.astype(jnp.float32)
    masked = increments * wet_float
    own_rows = lax.dynamic_slice_in_dim(vert_corr, lev_first, lev_dev, 1)
    correlated = jnp.einsum(
        "toh,dthxy->dtoxy",
        own_rows,
        lax.all_gather(masked, "lev", axis=2, tiled=True),
        precision=lax.Precision.HIGHEST,
    )
    field = correlated * wet_float
    total_y = cells_y * lax.axis_size("gy")
    local_rows = lax.axis_index("gy") * cells_y + jnp.arange(cells_y, dtype=jnp.int32)
    open_local = (local_rows != total_y - 1).astype(jnp.float32)
    east_local = kappa[0]
    north_local = kappa[1] * open_local[None, :]
    east_low = from_behind(east_local[-1:, :], "gx", 1)
    north_low = shifted(north_local[:, -1:], "gy", 1)
    zero_row = jnp.zeros((1, cells_y), jnp.float32)
    zero_col = jnp.zeros((cells_x, 1), jnp.float32)
    east_ext = jnp.pad(jnp.concatenate([east_low, east_local, zero_row], axis=0), ((0, 0), (1, 1)))
    north_ext = jnp.pad(
        jnp.concatenate([north_low, north_local, zero_col], axis=1), ((1, 1), (0, 0))
    )

    def one_pass(step, current):
        extended = padded(current, (("gx", 3), ("gy", 4)), 1)
        return relax(extended, east_ext, north_ext, wet_float)

    field = lax.fori_loop(0, PASSES, one_pass, field)
    return field


TILE = 8
LANES = 128
WIDTH = 5
MESH = pl.DeviceIdType.MESH


def remote(src, dst, send_sem, recv_sem, device):
    return pltpu.make_async_remote_copy(
        src_ref=src,
        dst_ref=dst,
        send_sem=send_sem,
        recv_sem=recv_sem,
        device_id=device,
        device_id_type=MESH,
    )


def kernel(
    inc_hbm, corr_hbm, kappa_hbm, sea_hbm, count_hbm, out_ref,
    inc_ref, corr_ref, kappa_ref, sea_ref, count_ref, masked_ref,
    geo, own, other, field, halo, east, north, south, stage,
    own_sems, same_sems, cross_sems, geo_sems, halo_sems, out_sems, in_sems, keep_sems,
):
    lev, gx, gy = lax.axis_index("lev"), lax.axis_index("gx"), lax.axis_index("gy")
    count = lax.axis_size("gx")
    cells = masked_ref.shape[1]
    levels = masked_ref.shape[2]
    lanes = masked_ref.shape[3]
    tiles = levels // TILE
    width = WIDTH
    rows = cells + 2 * width
    rounds = PASSES // width
    east_dev = {"gx": lax.rem(gx + 1, count)}
    west_dev = {"gx": lax.rem(gx + count - 1, count)}
    mate = {"gy": 1 - gy}
    pair = {"lev": 1 - lev}
    cross = {"lev": 1 - lev, "gy": 1 - gy}

    loads = [
        pltpu.make_async_copy(src, dst, in_sems.at[n])
        for n, (src, dst) in enumerate((
            (sea_hbm, sea_ref), (count_hbm, count_ref), (kappa_hbm, kappa_ref),
            (inc_hbm, inc_ref), (corr_hbm, corr_ref)))
    ]
    for load in loads:
        load.start()
    barrier = pltpu.get_barrier_semaphore()
    everyone = (east_dev, west_dev, mate, pair, cross)
    for device in everyone:
        pl.semaphore_signal(barrier, inc=1, device_id=device, device_id_type=MESH)
    columns = gy * lanes + lax.broadcasted_iota(jnp.int32, (1, lanes), 1)
    is_open = (columns != lanes * lax.axis_size("gy") - 1).astype(jnp.float32)
    for load in loads:
        load.wait()
    number = lev * levels + lax.broadcasted_iota(jnp.int32, (levels, lanes), 0)
    for x in range(cells):
        sea = sea_ref[pl.ds(x, levels, stride=cells), :]
        value = jnp.where(number < count_ref[x:x + 1, :], sea, 0).astype(jnp.float32)
        geo[gy, width + x, 0:levels] = value
        for t in range(2):
            masked_ref[t, x] = inc_ref[t, pl.ds(x, levels, stride=cells), :] * value
        geo[gy, width + x, levels:levels + 1] = kappa_ref[0, x:x + 1]
        geo[gy, width + x, levels + 1:levels + 2] = kappa_ref[1, x:x + 1] * is_open
        geo[gy, width + x, levels + 2:] = jnp.zeros((TILE - 2, lanes), jnp.float32)
    pl.semaphore_wait(barrier, len(everyone))

    starts = ((0, width), (cells - width, width), (width, cells - 2 * width))
    own_copies, same_copies, cross_copies = [], [], []
    for q, (start, size) in enumerate(starts):
        span = pl.ds(start, size)
        own_copies.append(remote(
            masked_ref.at[1 - gy, span], own.at[span], own_sems.at[0, q], own_sems.at[1, q], mate))
        same_copies.append(remote(
            masked_ref.at[gy, span], other.at[gy, span],
            same_sems.at[0, q], same_sems.at[1, q], pair))
        cross_copies.append(remote(
            masked_ref.at[1 - gy, span], other.at[gy, span],
            cross_sems.at[0, q], cross_sems.at[1, q], cross))
    geo_copies = [
        remote(geo.at[gy, pl.ds(width, cells)], geo.at[gy, pl.ds(width, cells)], geo_sems.at[0, 0], geo_sems.at[1, 0], mate),
        remote(geo.at[gy, pl.ds(cells, width)],
               geo.at[gy, pl.ds(0, width)],
               geo_sems.at[0, 1], geo_sems.at[1, 1], east_dev),
        remote(geo.at[gy, pl.ds(width, width)],
               geo.at[gy, pl.ds(width + cells, width)],
               geo_sems.at[0, 2], geo_sems.at[1, 2], west_dev),
    ]
    for q in range(len(starts)):
        same_copies[q].start()
        cross_copies[q].start()
        own_copies[q].start()
        if q == 0:
            for copy in geo_copies:
                copy.start()

    mine = corr_ref[gy, pl.ds(pl.multiple_of(lev * levels, TILE), levels), :]
    swapped = jnp.concatenate([mine[:, levels:], mine[:, :levels]], axis=1)
    corr = jnp.where(lev == 0, mine, swapped)
    high = corr.astype(jnp.bfloat16)
    low = (corr - high.astype(jnp.float32)).astype(jnp.bfloat16)
    weights = jnp.concatenate([high, high, low], axis=1)

    def halo_copies(r, k):
        return (
            remote(field.at[k, pl.ds(width, width)], halo.at[r, 1, k],
                   halo_sems.at[0, r, 0, k], halo_sems.at[1, r, 0, k], west_dev),
            remote(field.at[k, pl.ds(cells, width)], halo.at[r, 0, k],
                   halo_sems.at[0, r, 1, k], halo_sems.at[1, r, 1, k], east_dev),
        )

    def vertical(x):
        mine = masked_ref[gy, x]
        theirs = own[x]
        first = jnp.where(gy == 0, mine, theirs)
        second = jnp.where(gy == 0, theirs, mine)
        near = jnp.concatenate([first, second], axis=1)
        far = jnp.concatenate([other[0, x], other[1, x]], axis=1)
        both = jnp.concatenate([near, far], axis=0)
        top = both.astype(jnp.bfloat16)
        rest = (both - top.astype(jnp.float32)).astype(jnp.bfloat16)
        stack = jnp.concatenate([top, rest, top], axis=0)
        result = jnp.dot(weights, stack, preferred_element_type=jnp.float32)
        for half in range(2):
            for k in range(tiles):
                value = result[k * TILE:(k + 1) * TILE, half * LANES:(half + 1) * LANES]
                wet = geo[half, width + x, k * TILE:(k + 1) * TILE]
                field[k, width + x, half] = value * wet

    pending = [halo_copies(0, k) for k in range(tiles)]
    forward = []
    geo_copies[0].wait()
    for q, (start, size) in enumerate(starts):
        own_copies[q].wait()
        same_copies[q].wait()
        cross_copies[q].wait()
        for x in range(start, start + size):
            vertical(x)
        if q < 2:
            for k in range(tiles):
                pending[k][q].start()
        if q == 1:
            for side, place in ((1, 0), (2, width + cells)):
                geo_copies[side].wait()
                edge = geo.at[gy, pl.ds(place, width)]
                forward.append(remote(
                    edge, edge, geo_sems.at[0, 2 + side], geo_sems.at[1, 2 + side], mate))
                forward[-1].start()
    for copy in forward:
        copy.wait()
    for half in range(2):
        for row in range(rows):
            east[row, half] = jnp.broadcast_to(geo[half, row, levels:levels + 1], (TILE, LANES))
            north[row, half] = jnp.broadcast_to(geo[half, row, levels + 1:levels + 2], (TILE, LANES))

    lane = lax.broadcasted_iota(jnp.int32, (TILE, LANES), 1)
    at_end = lane == LANES - 1
    at_start = lane == 0
    for row in range(rows):
        moved = [pltpu.roll(north[row, h], 1, 1) for h in range(2)]
        south[row, 0] = jnp.where(at_start, moved[1], moved[0])
        south[row, 1] = jnp.where(at_start, moved[0], moved[1])

    def relax_tile(r, k):
        for step in range(width):
            def row_of(row):
                if step == 0 and row < width:
                    return halo[r, 0, k, row, 0], halo[r, 0, k, row, 1]
                if step == 0 and row >= width + cells:
                    at = row - width - cells
                    return halo[r, 1, k, at, 0], halo[r, 1, k, at, 1]
                return field[k, row, 0], field[k, row, 1]

            first, last = step + 1, rows - 2 - step
            before, here = row_of(first - 1), row_of(first)
            flux = [east[first - 1, h] * (here[h] - before[h]) for h in range(2)]
            for row in range(first, last + 1):
                after = row_of(row + 1)
                turned = [pltpu.roll(here[h], LANES - 1, 1) for h in range(2)]
                up = [jnp.where(at_end, turned[1], turned[0]), turned[1]]
                back = [pltpu.roll(here[h], 1, 1) for h in range(2)]
                below = [back[0], jnp.where(at_start, back[0], back[1])]
                rise = [north[row, h] * (up[h] - here[h]) for h in range(2)]
                down = [south[row, h] * (here[h] - below[h]) for h in range(2)]
                ahead = [east[row, h] * (after[h] - here[h]) for h in range(2)]
                for h in range(2):
                    wet = geo[h, row, k * TILE:(k + 1) * TILE]
                    total = here[h] + ((ahead[h] - flux[h]) + (rise[h] - down[h]))
                    if r == rounds - 1 and step == width - 1:
                        stage[k, h, pl.ds(row - width, TILE, stride=cells), :] = wet * total
                    else:
                        field[k, row, h] = wet * total
                here, flux = after, ahead

    out_copies = []
    for r in range(rounds):
        later = []
        for k in range(tiles):
            for copy in pending[k]:
                copy.wait()
            relax_tile(r, k)
            if r < rounds - 1:
                later.append(halo_copies(r + 1, k))
                for copy in later[-1]:
                    copy.start()
            else:
                out_copies.append(remote(
                    stage.at[k, 1 - gy], out_ref.at[gy, k],
                    out_sems.at[0, k], out_sems.at[1, k], mate))
                out_copies[-1].start()
                out_copies.append(pltpu.make_async_copy(
                    stage.at[k, gy], out_ref.at[gy, k], keep_sems.at[k]))
                out_copies[-1].start()
        pending = later
    for copy in out_copies:
        copy.wait()


def fused(increments, vert_corr, kappa, sea_mask, level_count):
    levels, cells, lanes = sea_mask.shape
    tiles = levels // TILE
    width = WIDTH
    rows = cells + 2 * width
    rounds = PASSES // width
    hbm = pl.BlockSpec(memory_space=pl.ANY)
    f32 = jnp.float32
    dma = pltpu.SemaphoreType.DMA
    result = pl.pallas_call(
        kernel,
        out_shape=jax.ShapeDtypeStruct((2, tiles, TILE * cells, lanes), f32),
        in_specs=[hbm] * 5,
        out_specs=pl.BlockSpec(memory_space=pltpu.VMEM),
        scratch_shapes=[
            pltpu.VMEM((2, levels * cells, lanes), f32),
            pltpu.VMEM(vert_corr.shape, f32),
            pltpu.VMEM(kappa.shape, f32),
            pltpu.VMEM((levels * cells, lanes), sea_mask.dtype),
            pltpu.VMEM(level_count.shape, level_count.dtype),
            pltpu.VMEM((2, cells, levels, lanes), f32),
            pltpu.VMEM((2, rows, levels + TILE, lanes), f32),
            pltpu.VMEM((cells, levels, lanes), f32),
            pltpu.VMEM((2, cells, levels, lanes), f32),
            pltpu.VMEM((tiles, rows, 2, TILE, lanes), f32),
            pltpu.VMEM((rounds, 2, tiles, width, 2, TILE, lanes), f32),
            pltpu.VMEM((rows, 2, TILE, lanes), f32),
            pltpu.VMEM((rows, 2, TILE, lanes), f32),
            pltpu.VMEM((rows, 2, TILE, lanes), f32),
            pltpu.VMEM((tiles, 2, TILE * cells, lanes), f32),
            dma((2, 3)),
            dma((2, 3)),
            dma((2, 3)),
            dma((2, 5)),
            dma((2, rounds, 2, tiles)),
            dma((2, tiles)),
            dma((5,)),
            dma((tiles,)),
        ],
        compiler_params=pltpu.CompilerParams(
            collective_id=0, has_side_effects=True, vmem_limit_bytes=32 * 1024 * 1024
        ),
        cost_estimate=pl.CostEstimate(flops=60_000_000, bytes_accessed=4_000_000, transcendentals=0),
    )(
        *(pltpu.with_memory_space_constraint(v, pltpu.HBM) for v in (
            increments.reshape(2, levels * cells, lanes), vert_corr, kappa,
            sea_mask.reshape(levels * cells, lanes), level_count))
    )
    return result.reshape(increments.shape)


def fits(mesh):
    shape = mesh.shape
    return shape["lev"] == 2 and shape["gy"] == 2 and shape["gx"] > 2


def solution(mesh):
    in_specs = (
        P(None, None, "lev", "gx", "gy"),
        P(),
        P(None, "gx", "gy"),
        P("lev", "gx", "gy"),
        P("gx", "gy"),
    )
    out_specs = P(None, None, "lev", "gx", "gy")
    return jax.shard_map(
        fused if fits(mesh) else per_device, mesh=mesh, in_specs=in_specs, out_specs=out_specs, check_vma=False
    )
```

```python
import jax
import jax.numpy as jnp
from jax import lax
from jax.experimental import pallas as pl
from jax.experimental.pallas import tpu as pltpu
from jax.sharding import PartitionSpec as P

PASSES = 10


def from_behind(block, axis, distance):
    devices = range(lax.axis_size(axis))
    route = [((i - distance) % len(devices), i) for i in devices]
    return lax.ppermute(block, axis, route)


def shifted(block, axis, distance):
    devices = range(lax.axis_size(axis))
    route = [(i - distance, i) for i in devices if i - distance in devices]
    return lax.ppermute(block, axis, route)


def padded(cells, sides, width):
    for axis, dim in sides:
        count = lax.axis_size(axis)
        head = lax.slice_in_dim(cells, 0, width, axis=dim)
        tail = lax.slice_in_dim(cells, cells.shape[dim] - width, cells.shape[dim], axis=dim)
        cells = jnp.concatenate(
            [
                lax.ppermute(tail, axis, [(i, (i + 1) % count) for i in range(count)]),
                cells,
                lax.ppermute(head, axis, [((i + 1) % count, i) for i in range(count)]),
            ],
            axis=dim,
        )
    return cells


def relax(extended, east_ext, north_ext, wet_center):
    center = extended[..., 1:-1, 1:-1]
    flux = east_ext[1:-1, 1:-1] * (extended[..., 2:, 1:-1] - center)
    flux = flux + east_ext[:-2, 1:-1] * (extended[..., :-2, 1:-1] - center)
    flux = flux + north_ext[1:-1, 1:-1] * (extended[..., 1:-1, 2:] - center)
    flux = flux + north_ext[1:-1, :-2] * (extended[..., 1:-1, :-2] - center)
    return wet_center * (center + flux)


def per_device(increments, vert_corr, kappa, sea_mask, level_count):
    lev_dev = sea_mask.shape[0]
    cells_x = sea_mask.shape[1]
    cells_y = sea_mask.shape[2]
    lev_first = lax.axis_index("lev") * lev_dev
    levels = lev_first + jnp.arange(lev_dev, dtype=jnp.int32)
    wet = sea_mask * (levels[:, None, None] < level_count[None]).astype(jnp.int32)
    wet_float = wet.astype(jnp.float32)
    masked = increments * wet_float
    own_rows = lax.dynamic_slice_in_dim(vert_corr, lev_first, lev_dev, 1)
    correlated = jnp.einsum(
        "toh,dthxy->dtoxy",
        own_rows,
        lax.all_gather(masked, "lev", axis=2, tiled=True),
        precision=lax.Precision.HIGHEST,
    )
    field = correlated * wet_float
    total_y = cells_y * lax.axis_size("gy")
    local_rows = lax.axis_index("gy") * cells_y + jnp.arange(cells_y, dtype=jnp.int32)
    open_local = (local_rows != total_y - 1).astype(jnp.float32)
    east_local = kappa[0]
    north_local = kappa[1] * open_local[None, :]
    east_low = from_behind(east_local[-1:, :], "gx", 1)
    north_low = shifted(north_local[:, -1:], "gy", 1)
    zero_row = jnp.zeros((1, cells_y), jnp.float32)
    zero_col = jnp.zeros((cells_x, 1), jnp.float32)
    east_ext = jnp.pad(jnp.concatenate([east_low, east_local, zero_row], axis=0), ((0, 0), (1, 1)))
    north_ext = jnp.pad(
        jnp.concatenate([north_low, north_local, zero_col], axis=1), ((1, 1), (0, 0))
    )

    def one_pass(step, current):
        extended = padded(current, (("gx", 3), ("gy", 4)), 1)
        return relax(extended, east_ext, north_ext, wet_float)

    field = lax.fori_loop(0, PASSES, one_pass, field)
    return field


TILE = 8
LANES = 128
WIDTH = 5
MESH = pl.DeviceIdType.MESH


def remote(src, dst, send_sem, recv_sem, device):
    return pltpu.make_async_remote_copy(
        src_ref=src,
        dst_ref=dst,
        send_sem=send_sem,
        recv_sem=recv_sem,
        device_id=device,
        device_id_type=MESH,
    )


def kernel(
    inc_hbm, corr_hbm, kappa_hbm, sea_hbm, count_hbm, out_ref,
    inc_ref, corr_ref, kappa_ref, sea_ref, count_ref, masked_ref,
    geo, own, other, field, halo, east, north, south, stage,
    own_sems, same_sems, cross_sems, geo_sems, halo_sems, out_sems, in_sems, keep_sems,
):
    lev, gx, gy = lax.axis_index("lev"), lax.axis_index("gx"), lax.axis_index("gy")
    count = lax.axis_size("gx")
    cells = masked_ref.shape[1]
    levels = masked_ref.shape[2]
    lanes = masked_ref.shape[3]
    tiles = levels // TILE
    width = WIDTH
    rows = cells + 2 * width
    rounds = PASSES // width
    east_dev = {"gx": lax.rem(gx + 1, count)}
    west_dev = {"gx": lax.rem(gx + count - 1, count)}
    mate = {"gy": 1 - gy}
    pair = {"lev": 1 - lev}
    cross = {"lev": 1 - lev, "gy": 1 - gy}

    loads = [
        pltpu.make_async_copy(src, dst, in_sems.at[n])
        for n, (src, dst) in enumerate((
            (sea_hbm, sea_ref), (count_hbm, count_ref), (kappa_hbm, kappa_ref),
            (inc_hbm, inc_ref), (corr_hbm, corr_ref)))
    ]
    for load in loads:
        load.start()
    barrier = pltpu.get_barrier_semaphore()
    everyone = (east_dev, west_dev, mate, pair, cross)
    for device in everyone:
        pl.semaphore_signal(barrier, inc=1, device_id=device, device_id_type=MESH)
    columns = gy * lanes + lax.broadcasted_iota(jnp.int32, (1, lanes), 1)
    is_open = (columns != lanes * lax.axis_size("gy") - 1).astype(jnp.float32)
    for load in loads:
        load.wait()
    number = lev * levels + lax.broadcasted_iota(jnp.int32, (levels, lanes), 0)
    for x in range(cells):
        sea = sea_ref[pl.ds(x, levels, stride=cells), :]
        value = jnp.where(number < count_ref[x:x + 1, :], sea, 0).astype(jnp.float32)
        geo[gy, width + x, 0:levels] = value
        for t in range(2):
            masked_ref[t, x] = inc_ref[t, pl.ds(x, levels, stride=cells), :] * value
        geo[gy, width + x, levels:levels + 1] = kappa_ref[0, x:x + 1]
        geo[gy, width + x, levels + 1:levels + 2] = kappa_ref[1, x:x + 1] * is_open
        geo[gy, width + x, levels + 2:] = jnp.zeros((TILE - 2, lanes), jnp.float32)
    pl.semaphore_wait(barrier, len(everyone))

    middle = (cells - 2 * width) // 2
    starts = (
        (0, width), (cells - width, width), (width, middle), (width + middle, cells - 2 * width - middle))
    own_copies, same_copies, cross_copies = [], [], []
    for q, (start, size) in enumerate(starts):
        span = pl.ds(start, size)
        own_copies.append(remote(
            masked_ref.at[1 - gy, span], own.at[span], own_sems.at[0, q], own_sems.at[1, q], mate))
        same_copies.append(remote(
            masked_ref.at[gy, span], other.at[gy, span],
            same_sems.at[0, q], same_sems.at[1, q], pair))
        cross_copies.append(remote(
            masked_ref.at[1 - gy, span], other.at[gy, span],
            cross_sems.at[0, q], cross_sems.at[1, q], cross))
    geo_copies = [
        remote(geo.at[gy, pl.ds(width, cells)], geo.at[gy, pl.ds(width, cells)], geo_sems.at[0, 0], geo_sems.at[1, 0], mate),
        remote(geo.at[gy, pl.ds(cells, width)],
               geo.at[gy, pl.ds(0, width)],
               geo_sems.at[0, 1], geo_sems.at[1, 1], east_dev),
        remote(geo.at[gy, pl.ds(width, width)],
               geo.at[gy, pl.ds(width + cells, width)],
               geo_sems.at[0, 2], geo_sems.at[1, 2], west_dev),
    ]
    for copy in geo_copies[1:]:
        copy.start()
    geo_copies[0].start()
    for q in range(len(starts)):
        same_copies[q].start()
        cross_copies[q].start()
        own_copies[q].start()

    mine = corr_ref[gy, pl.ds(pl.multiple_of(lev * levels, TILE), levels), :]
    swapped = jnp.concatenate([mine[:, levels:], mine[:, :levels]], axis=1)
    corr = jnp.where(lev == 0, mine, swapped)
    high = corr.astype(jnp.bfloat16)
    low = (corr - high.astype(jnp.float32)).astype(jnp.bfloat16)
    weights = jnp.concatenate([high, high, low], axis=1)

    def halo_copies(r, k):
        return (
            remote(field.at[k, pl.ds(width, width)], halo.at[r, 1, k],
                   halo_sems.at[0, r, 0, k], halo_sems.at[1, r, 0, k], west_dev),
            remote(field.at[k, pl.ds(cells, width)], halo.at[r, 0, k],
                   halo_sems.at[0, r, 1, k], halo_sems.at[1, r, 1, k], east_dev),
        )

    def vertical(x):
        mine = masked_ref[gy, x]
        theirs = own[x]
        first = jnp.where(gy == 0, mine, theirs)
        second = jnp.where(gy == 0, theirs, mine)
        near = jnp.concatenate([first, second], axis=1)
        far = jnp.concatenate([other[0, x], other[1, x]], axis=1)
        both = jnp.concatenate([near, far], axis=0)
        top = both.astype(jnp.bfloat16)
        rest = (both - top.astype(jnp.float32)).astype(jnp.bfloat16)
        stack = jnp.concatenate([top, rest, top], axis=0)
        result = jnp.dot(weights, stack, preferred_element_type=jnp.float32)
        for half in range(2):
            for k in range(tiles):
                value = result[k * TILE:(k + 1) * TILE, half * LANES:(half + 1) * LANES]
                wet = geo[half, width + x, k * TILE:(k + 1) * TILE]
                field[k, width + x, half] = value * wet

    pending = [halo_copies(0, k) for k in range(tiles)]
    forward = []
    geo_copies[0].wait()
    for q, (start, size) in enumerate(starts):
        own_copies[q].wait()
        same_copies[q].wait()
        cross_copies[q].wait()
        for x in range(start, start + size):
            vertical(x)
        if q < 2:
            for k in range(tiles):
                pending[k][q].start()
        if q == 1:
            for side, place in ((1, 0), (2, width + cells)):
                geo_copies[side].wait()
                edge = geo.at[gy, pl.ds(place, width)]
                forward.append(remote(
                    edge, edge, geo_sems.at[0, 2 + side], geo_sems.at[1, 2 + side], mate))
                forward[-1].start()
    for copy in forward:
        copy.wait()
    for half in range(2):
        for row in range(rows):
            east[row, half] = jnp.broadcast_to(geo[half, row, levels:levels + 1], (TILE, LANES))
            north[row, half] = jnp.broadcast_to(geo[half, row, levels + 1:levels + 2], (TILE, LANES))

    lane = lax.broadcasted_iota(jnp.int32, (TILE, LANES), 1)
    at_end = lane == LANES - 1
    at_start = lane == 0
    for row in range(rows):
        moved = [pltpu.roll(north[row, h], 1, 1) for h in range(2)]
        south[row, 0] = jnp.where(at_start, moved[1], moved[0])
        south[row, 1] = jnp.where(at_start, moved[0], moved[1])

    def relax_tile(r, k):
        for step in range(width):
            def row_of(row):
                if step == 0 and row < width:
                    return halo[r, 0, k, row, 0], halo[r, 0, k, row, 1]
                if step == 0 and row >= width + cells:
                    at = row - width - cells
                    return halo[r, 1, k, at, 0], halo[r, 1, k, at, 1]
                return field[k, row, 0], field[k, row, 1]

            first, last = step + 1, rows - 2 - step
            before, here = row_of(first - 1), row_of(first)
            flux = [east[first - 1, h] * (here[h] - before[h]) for h in range(2)]
            for row in range(first, last + 1):
                after = row_of(row + 1)
                turned = [pltpu.roll(here[h], LANES - 1, 1) for h in range(2)]
                up = [jnp.where(at_end, turned[1], turned[0]), turned[1]]
                back = [pltpu.roll(here[h], 1, 1) for h in range(2)]
                below = [back[0], jnp.where(at_start, back[0], back[1])]
                rise = [north[row, h] * (up[h] - here[h]) for h in range(2)]
                down = [south[row, h] * (here[h] - below[h]) for h in range(2)]
                ahead = [east[row, h] * (after[h] - here[h]) for h in range(2)]
                for h in range(2):
                    wet = geo[h, row, k * TILE:(k + 1) * TILE]
                    total = here[h] + ((ahead[h] - flux[h]) + (rise[h] - down[h]))
                    if r == rounds - 1 and step == width - 1:
                        stage[k, h, pl.ds(row - width, TILE, stride=cells), :] = wet * total
                    else:
                        field[k, row, h] = wet * total
                here, flux = after, ahead

    out_copies = []
    for r in range(rounds):
        later = []
        for k in range(tiles):
            for copy in pending[k]:
                copy.wait()
            relax_tile(r, k)
            if r < rounds - 1:
                later.append(halo_copies(r + 1, k))
                for copy in later[-1]:
                    copy.start()
            else:
                out_copies.append(remote(
                    stage.at[k, 1 - gy], out_ref.at[gy, k],
                    out_sems.at[0, k], out_sems.at[1, k], mate))
                out_copies[-1].start()
                out_copies.append(pltpu.make_async_copy(
                    stage.at[k, gy], out_ref.at[gy, k], keep_sems.at[k]))
                out_copies[-1].start()
        pending = later
    for copy in out_copies:
        copy.wait()


def fused(increments, vert_corr, kappa, sea_mask, level_count):
    levels, cells, lanes = sea_mask.shape
    tiles = levels // TILE
    width = WIDTH
    rows = cells + 2 * width
    rounds = PASSES // width
    hbm = pl.BlockSpec(memory_space=pl.ANY)
    f32 = jnp.float32
    dma = pltpu.SemaphoreType.DMA
    result = pl.pallas_call(
        kernel,
        out_shape=jax.ShapeDtypeStruct((2, tiles, TILE * cells, lanes), f32),
        in_specs=[hbm] * 5,
        out_specs=pl.BlockSpec(memory_space=pltpu.VMEM),
        scratch_shapes=[
            pltpu.VMEM((2, levels * cells, lanes), f32),
            pltpu.VMEM(vert_corr.shape, f32),
            pltpu.VMEM(kappa.shape, f32),
            pltpu.VMEM((levels * cells, lanes), sea_mask.dtype),
            pltpu.VMEM(level_count.shape, level_count.dtype),
            pltpu.VMEM((2, cells, levels, lanes), f32),
            pltpu.VMEM((2, rows, levels + TILE, lanes), f32),
            pltpu.VMEM((cells, levels, lanes), f32),
            pltpu.VMEM((2, cells, levels, lanes), f32),
            pltpu.VMEM((tiles, rows, 2, TILE, lanes), f32),
            pltpu.VMEM((rounds, 2, tiles, width, 2, TILE, lanes), f32),
            pltpu.VMEM((rows, 2, TILE, lanes), f32),
            pltpu.VMEM((rows, 2, TILE, lanes), f32),
            pltpu.VMEM((rows, 2, TILE, lanes), f32),
            pltpu.VMEM((tiles, 2, TILE * cells, lanes), f32),
            dma((2, 4)),
            dma((2, 4)),
            dma((2, 4)),
            dma((2, 5)),
            dma((2, rounds, 2, tiles)),
            dma((2, tiles)),
            dma((5,)),
            dma((tiles,)),
        ],
        compiler_params=pltpu.CompilerParams(
            collective_id=0, has_side_effects=True, vmem_limit_bytes=32 * 1024 * 1024
        ),
        cost_estimate=pl.CostEstimate(flops=60_000_000, bytes_accessed=4_000_000, transcendentals=0),
    )(
        *(pltpu.with_memory_space_constraint(v, pltpu.HBM) for v in (
            increments.reshape(2, levels * cells, lanes), vert_corr, kappa,
            sea_mask.reshape(levels * cells, lanes), level_count))
    )
    return result.reshape(increments.shape)


def fits(mesh):
    shape = mesh.shape
    return shape["lev"] == 2 and shape["gy"] == 2 and shape["gx"] > 2


def solution(mesh):
    in_specs = (
        P(None, None, "lev", "gx", "gy"),
        P(),
        P(None, "gx", "gy"),
        P("lev", "gx", "gy"),
        P("gx", "gy"),
    )
    out_specs = P(None, None, "lev", "gx", "gy")
    return jax.shard_map(
        fused if fits(mesh) else per_device, mesh=mesh, in_specs=in_specs, out_specs=out_specs, check_vma=False
    )
```
